256 devices in a mesh: lat: 8 (over y, x_lo), lon: 32 (over z, x_hi, core).
Axes of the slice: x: 4 (x_hi: 2, x_lo: 2; x = x_hi * 2 + x_lo), y: 4, z: 8, core: 2. Of those that a mesh axis runs over, the one named last changes fastest.
Arguments:
- tokens: bfloat16 [4, 144, 768, 512], P(None, 'lat', 'lon'), may hold values from -6 to 6
- lat_shift: int32 [1], replicated, may hold values from 1 to 5
- lon_shift: int32 [1], replicated, may hold values from 1 to 11
- lat_valid: int32 [144], replicated, may hold values from 0 to 1, as said below
- ln1_gain: float32 [512], replicated, may hold values from 0.1 to 1.9
- ln1_bias: float32 [512], replicated, may hold values from -3 to 3
- w_qkv: bfloat16 [512, 1536], replicated
- w_proj: bfloat16 [512, 512], replicated, may hold values from -0.25 to 0.25
- b_proj: float32 [512], replicated, may hold values from -3 to 3
- ln2_gain: float32 [512], replicated, may hold values from 0.1 to 1.9
- ln2_bias: float32 [512], replicated, may hold values from -3 to 3
- w_fc1: bfloat16 [512, 2048], replicated, may hold values from -0.25 to 0.25
- b_fc1: float32 [2048], replicated, may hold values from -3 to 3
- w_fc2: bfloat16 [2048, 512], replicated, may hold values from -0.125 to 0.125
- b_fc2: float32 [512], replicated, may hold values from -3 to 3
- merge_gain: float32 [2048], replicated, may hold values from 0.1 to 1.9
- merge_bias: float32 [2048], replicated, may hold values from -3 to 3
- w_merge: bfloat16 [2048, 1024], replicated, may hold values from -0.125 to 0.125
Outputs:
- merged: bfloat16 [4, 72, 384, 1024], P(None, 'lat', 'lon')
The draws below stay inside these ranges and needn't reach their ends.
Inputs may be any that keep to these rules, and one draw needn't show every extreme that they name: lat_valid is 0 on the first 0 to 5 rows and on the last 1 to 18 rows of the grid, and 1 on every row between.
All inputs are finite; a program needn't handle non-finite values.
Results may differ from the reference program's by a relative error of at most 0.012.
Values may be sent and summed in bfloat16 or wider, within the bound.
A program may use at most 192 MiB of HBM per device.

```python
import math
import jax
import jax.numpy as jnp
from jax import lax

D = 512
HEADS = 8
FF = 2048
LEVELS = 4
WIN_LAT = 6
WIN_LON = 12
LAT_DEV = 18
NLAT = 144
NLON = 768


def draw_lat_valid(key, part):
    key = jax.random.fold_in(key, 5)
    key_top, key_bottom = jax.random.split(key)
    top_padded = jax.random.randint(key_top, (), 0, WIN_LAT)
    bottom_padded = jax.random.randint(key_bottom, (), 1, LAT_DEV + 1)
    row_index = jnp.arange(NLAT, dtype=jnp.int32)
    inside = (row_index >= top_padded) & (row_index < NLAT - bottom_padded)
    return inside.astype(jnp.int32)


def draw_w_qkv(key, part):
    key = jax.random.fold_in(key, 11)
    key_base = jax.random.fold_in(key, 0)
    base = jax.random.normal(key_base, (D, 3 * D), jnp.float32) * (1.0 / math.sqrt(D))
    return base.astype(jnp.bfloat16)


def steps_of(rng, extent, shards, smallest, top_value):
    factor_of = 1.0
    for position, shards_of in shards:
        steps = jax.random.uniform(jax.random.fold_in(jax.random.fold_in(rng, 6), position), (shards_of,), jnp.float32, smallest / len(shards), top_value / len(shards))
        factor_of = factor_of * jnp.repeat(jnp.exp(steps), extent[position] // shards_of).reshape((-1,) + (1,) * (len(extent) - 1 - position))
    return factor_of


def gaussian(own_key, dims, width, reach, shards=(), kind=jnp.bfloat16):
    array = jax.random.normal(own_key, dims, jnp.float32) * width
    if len(shards) > 0:
        array = steps_of(own_key, dims, shards, -0.22, 0.18) * array
    return jnp.clip(array, min=-reach, max=reach).astype(kind)


def setup_inputs(seed: int = 0) -> dict:
    key_of = jax.random.split(jax.random.key(seed), 19)
    tokens = gaussian(key_of[0], (LEVELS, NLAT, NLON, D), 1.0, 6.0, ((1, 8), (2, 32)))
    lat_shift = jax.random.randint(key_of[1], (1,), 1, WIN_LAT).astype(jnp.int32)
    lon_shift = jax.random.randint(key_of[2], (1,), 1, WIN_LON).astype(jnp.int32)
    lat_valid = draw_lat_valid(jax.random.fold_in(key_of[18], 71), 0)
    ln1_gain = jnp.clip(1.0 + 0.18 * jax.random.normal(key_of[4], (D,), jnp.float32), 0.1, 1.9)
    ln1_bias = gaussian(key_of[5], (D,), 0.5, 3.0, (), jnp.float32)
    w_qkv = draw_w_qkv(jax.random.fold_in(key_of[18], 71), 0)
    w_proj = gaussian(key_of[7], (D, D), D ** -0.5, 0.25)
    b_proj = gaussian(key_of[8], (D,), 0.5, 3.0, (), jnp.float32)
    ln2_gain = jnp.clip(1.0 + 0.18 * jax.random.normal(key_of[9], (D,), jnp.float32), 0.1, 1.9)
    ln2_bias = gaussian(key_of[10], (D,), 0.5, 3.0, (), jnp.float32)
    w_fc1 = gaussian(key_of[11], (D, FF), D ** -0.5, 0.25)
    b_fc1 = gaussian(key_of[12], (FF,), 0.5, 3.0, (), jnp.float32)
    w_fc2 = gaussian(key_of[13], (FF, D), FF ** -0.5, 0.125)
    b_fc2 = gaussian(key_of[14], (D,), 0.5, 3.0, (), jnp.float32)
    merge_gain = jnp.clip(1.0 + 0.18 * jax.random.normal(key_of[15], (4 * D,), jnp.float32), 0.1, 1.9)
    merge_bias = gaussian(key_of[16], (4 * D,), 0.5, 3.0, (), jnp.float32)
    w_merge = gaussian(key_of[17], (4 * D, 2 * D), (4 * D) ** -0.5, 0.125)
    return dict(tokens=tokens, lat_shift=lat_shift, lon_shift=lon_shift, lat_valid=lat_valid, ln1_gain=ln1_gain, ln1_bias=ln1_bias, w_qkv=w_qkv, w_proj=w_proj, b_proj=b_proj, ln2_gain=ln2_gain, ln2_bias=ln2_bias, w_fc1=w_fc1, b_fc1=b_fc1, w_fc2=w_fc2, b_fc2=b_fc2, merge_gain=merge_gain, merge_bias=merge_bias, w_merge=w_merge)


NORM_EPS = 1e-05

def layer_norm(inputs, gain_vec, bias_vec):
    inputs = inputs.astype(jnp.float32)
    row_mean = lax.optimization_barrier(jnp.mean(inputs, axis=-1, keepdims=True))
    centred = inputs - row_mean
    row_var = lax.optimization_barrier(jnp.mean(centred * centred, axis=-1, keepdims=True))
    return centred * lax.rsqrt(row_var + NORM_EPS) * gain_vec + bias_vec

def to_windows(blocks):
    levels, lat_rows, lon_cols, feature = blocks.shape
    blocks = blocks.reshape(levels, lat_rows // WIN_LAT, WIN_LAT, lon_cols // WIN_LON, WIN_LON, feature)
    blocks = blocks.transpose(1, 3, 0, 2, 4, 5)
    return blocks.reshape(lat_rows // WIN_LAT, lon_cols // WIN_LON, levels * WIN_LAT * WIN_LON, feature)

def from_windows(windows, levels):
    band_count, sector_count, window_tokens, feature = windows.shape
    blocks = windows.reshape(band_count, sector_count, levels, WIN_LAT, WIN_LON, feature)
    blocks = blocks.transpose(2, 0, 3, 1, 4, 5)
    return blocks.reshape(levels, band_count * WIN_LAT, sector_count * WIN_LON, feature)

def window_attend(qkv_win, group_win, usable_win):
    qkv_win = lax.optimization_barrier(qkv_win)
    window_count, window_tokens, triple = qkv_win.shape
    model_width = triple // 3
    head_size = model_width // HEADS
    query_part = qkv_win[:, :, :model_width].astype(jnp.float32).reshape(window_count, window_tokens, HEADS, head_size)
    key_part = qkv_win[:, :, model_width:2 * model_width].astype(jnp.float32).reshape(window_count, window_tokens, HEADS, head_size)
    value_part = qkv_win[:, :, 2 * model_width:].astype(jnp.float32).reshape(window_count, window_tokens, HEADS, head_size)
    scores = jnp.einsum('nqhd,nkhd->nhqk', query_part, key_part) * (1.0 / math.sqrt(head_size))
    level_index = (jnp.arange(window_tokens, dtype=jnp.int32) // (WIN_LAT * WIN_LON) + 1) // 2
    same_level = level_index[:, None] == level_index[None, :]
    same_band = group_win[:, :, None] == group_win[:, None, :]
    itself = jnp.eye(window_tokens, dtype=bool)
    allowed = same_level[None] & same_band & (usable_win[:, None, :] | itself[None])
    scores = jnp.where(allowed[:, None], scores, -jnp.inf)
    row_top = lax.optimization_barrier(jnp.max(scores, axis=-1, keepdims=True))
    weights = jnp.exp(scores - row_top)
    weight_sum = lax.optimization_barrier(jnp.sum(weights, axis=-1, keepdims=True))
    probs = (weights / weight_sum).astype(jnp.bfloat16)
    probs = lax.optimization_barrier(probs)
    context = jnp.einsum('nhqk,nkhd->nqhd', probs.astype(jnp.float32), value_part)
    return context.reshape(window_count, window_tokens, model_width).astype(jnp.bfloat16)

def finish(base, context, w_proj, b_proj, ln2_gain, ln2_bias, w_fc1, b_fc1, w_fc2, b_fc2):
    levels, lat_rows, lon_cols, model_width = base.shape
    flat_base = base.reshape(-1, model_width)
    attended = jnp.dot(context.reshape(-1, model_width), w_proj, preferred_element_type=jnp.float32)
    residual = (flat_base.astype(jnp.float32) + attended + b_proj).astype(jnp.bfloat16)
    residual = lax.optimization_barrier(residual)
    normed = layer_norm(residual, ln2_gain, ln2_bias).astype(jnp.bfloat16)
    inner = jnp.dot(normed, w_fc1, preferred_element_type=jnp.float32) + b_fc1
    hidden = jax.nn.gelu(inner, approximate=False).astype(jnp.bfloat16)
    mixed = residual.astype(jnp.float32) + jnp.dot(hidden, w_fc2, preferred_element_type=jnp.float32) + b_fc2
    return mixed.astype(jnp.bfloat16).reshape(levels, lat_rows, lon_cols, model_width)

def merge_patches(mixed, merge_gain, merge_bias, w_merge):
    mixed = lax.optimization_barrier(mixed)
    levels, lat_rows, lon_cols, model_width = mixed.shape
    grouped = mixed.reshape(levels, lat_rows // 2, 2, lon_cols // 2, 2, model_width).transpose(0, 1, 3, 4, 2, 5)
    grouped = grouped.reshape(-1, 4 * model_width)
    normed = layer_norm(grouped, merge_gain, merge_bias).astype(jnp.bfloat16)
    merged = jnp.dot(normed, w_merge, preferred_element_type=jnp.float32)
    return merged.astype(jnp.bfloat16).reshape(levels, lat_rows // 2, lon_cols // 2, w_merge.shape[1])

def reference(tokens, lat_shift, lon_shift, lat_valid, ln1_gain, ln1_bias, w_qkv, w_proj, b_proj, ln2_gain, ln2_bias, w_fc1, b_fc1, w_fc2, b_fc2, merge_gain, merge_bias, w_merge):
    levels, lat_rows, lon_cols, model_width = tokens.shape
    row_shift = lat_shift[0]
    col_shift = lon_shift[0]
    normed = layer_norm(tokens, ln1_gain, ln1_bias).astype(jnp.bfloat16)
    qkv = jnp.dot(normed.reshape(-1, model_width), w_qkv, preferred_element_type=jnp.float32).astype(jnp.bfloat16)
    qkv = qkv.reshape(levels, lat_rows, lon_cols, 3 * model_width)
    rolled = jnp.roll(qkv, (-row_shift, -col_shift), axis=(1, 2))
    source_rows = (jnp.arange(lat_rows, dtype=jnp.int32) + row_shift) % lat_rows
    band_group = jnp.floor_divide(source_rows - row_shift, WIN_LAT)
    usable = lat_valid[source_rows] == 1
    group_map = jnp.broadcast_to(band_group[None, :, None, None], (levels, lat_rows, lon_cols, 1))
    usable_map = jnp.broadcast_to(usable[None, :, None, None], (levels, lat_rows, lon_cols, 1))
    qkv_win = to_windows(rolled)
    group_win = to_windows(group_map)[..., 0]
    usable_win = to_windows(usable_map)[..., 0]
    context_win = lax.map(lambda window_parts: window_attend(window_parts[0], window_parts[1], window_parts[2]), (qkv_win, group_win, usable_win))
    context = from_windows(context_win, levels)
    context = jnp.roll(context, (row_shift, col_shift), axis=(1, 2))
    mixed = finish(tokens, context, w_proj, b_proj, ln2_gain, ln2_bias, w_fc1, b_fc1, w_fc2, b_fc2)
    return merge_patches(mixed, merge_gain, merge_bias, w_merge)
```

```python
import functools

import jax
import jax.numpy as jnp
import numpy as np
from jax import lax
from jax.experimental import pallas as pl
from jax.experimental.pallas import tpu as pltpu
from jax.sharding import PartitionSpec as P

WIN_LAT = 6
WIN_LON = 12
UNIT = 144
HALF = 72
WIDTH = 512
FF = 2048
NORM_EPS = 1e-05
MESH = pl.DeviceIdType.MESH
BF16 = jnp.bfloat16
F32 = jnp.float32


def constants():
    rows = np.arange(UNIT)
    slot_i, slot_j = rows % HALF // WIN_LON, rows % WIN_LON
    block, within = rows // HALF, rows % HALF
    source = within // WIN_LON * 24 + block * WIN_LON + within % WIN_LON
    split = np.zeros((UNIT, UNIT), np.float32)
    split[rows, source] = 1.0
    gather = np.zeros((160, UNIT), np.float32)
    for part in range(4):
        col_odd, row_odd = part // 2, part % 2
        for row in range(3):
            for col in range(12):
                token = col // 6 * HALF + (2 * row + row_odd) * WIN_LON + 2 * (col % 6) + col_odd
                gather[part * 40 + row * 12 + col, token] = 1.0
    wide = np.ones((1, WIDTH), np.float32)
    grid = np.ones((UNIT, UNIT), np.float32)
    pairs = np.stack(
        (
            slot_i[:, None] * grid,
            slot_i[None, :] * grid,
            (rows[:, None] // HALF == rows[None, :] // HALF) * grid,
            np.eye(UNIT),
        )
    )
    return (
        jnp.asarray(split, BF16),
        jnp.asarray(gather, BF16),
        jnp.asarray(slot_i[:, None] * wide, BF16),
        jnp.asarray(slot_j[:, None] * wide, BF16),
        jnp.asarray(pairs, F32),
    )


def norm(values, gain, bias):
    mean = jnp.mean(values, axis=-1, keepdims=True)
    centred = values - mean
    var = jnp.mean(centred * centred, axis=-1, keepdims=True)
    return centred * lax.rsqrt(var + NORM_EPS) * gain + bias


def dot(left, right):
    return jnp.dot(left, right, preferred_element_type=F32)


def block_kernel(
    lats,
    lons,
    row_shift_ref,
    col_shift_ref,
    valid_ref,
    split_ref,
    gather_ref,
    slot_i_ref,
    slot_j_ref,
    pairs_ref,
    ln1_gain,
    ln1_bias,
    b_proj,
    ln2_gain,
    ln2_bias,
    b_fc1,
    b_fc2,
    merge_gain,
    merge_bias,
    x_hbm,
    w_qkv_hbm,
    w_proj_hbm,
    w_fc1_hbm,
    w_fc2_hbm,
    w_merge_hbm,
    out_ref,
    x_raw,
    w_qkv,
    w_proj,
    w_fc1,
    w_fc2,
    w_merge,
    tokens,
    normed,
    context,
    mixed,
    bias,
    qkv,
    grouped,
    x_sem,
    w_sem,
    in_lon_send,
    in_lon_recv,
    in_lat_send,
    in_lat_recv,
    in_diag_send,
    in_diag_recv,
    back_lon_send,
    back_lon_recv,
    back_lat_send,
    back_lat_recv,
    back_diag_send,
    back_diag_recv,
):
    lat, lon = lax.axis_index("lat"), lax.axis_index("lon")
    row_shift, col_shift = row_shift_ref[0], col_shift_ref[0]
    weights = [
        pltpu.make_async_copy(source, target, w_sem.at[place])
        for place, (source, target) in enumerate(
            (
                (w_qkv_hbm, w_qkv),
                (w_proj_hbm, w_proj),
                (w_fc1_hbm, w_fc1),
                (w_fc2_hbm, w_fc2),
                (w_merge_hbm, w_merge),
            )
        )
    ]

    def level_of(kind, half):
        return 1 + half + kind * (2 * half - 1)

    def x_copy(kind, half, band):
        level = level_of(kind, half)
        return pltpu.make_async_copy(
            x_hbm.at[level, band], x_raw.at[level, band], x_sem.at[level, band]
        )

    for step in range(3):
        for kind in range(2):
            for half in range(2):
                x_copy(kind, half, 2 - step if kind else step).start()
    for copy in weights:
        copy.start()

    def device(lat_step, lon_step):
        return {
            "lat": lax.rem(lat + lat_step + lats, lats),
            "lon": lax.rem(lon + lon_step + lons, lons),
        }

    def remote(ref, kind, source, target, send, recv, place):
        return pltpu.make_async_remote_copy(
            src_ref=ref.at[kind, source[0], source[1]],
            dst_ref=ref.at[kind, target[0], target[1]],
            send_sem=send,
            recv_sem=recv,
            device_id=place,
            device_id_type=MESH,
        )

    def in_lon(kind, band):
        return remote(
            normed,
            kind,
            (band + kind, 2 * kind),
            (band + kind, 2 - 2 * kind),
            in_lon_send.at[kind, band],
            in_lon_recv.at[kind, band],
            device(0, 2 * kind - 1),
        )

    def in_lat(kind, col):
        return remote(
            normed,
            kind,
            (3 * kind, col + kind),
            (3 - 3 * kind, col + kind),
            in_lat_send.at[kind, col],
            in_lat_recv.at[kind, col],
            device(2 * kind - 1, 0),
        )

    def in_diag(kind):
        return remote(
            normed,
            kind,
            (3 * kind, 2 * kind),
            (3 - 3 * kind, 2 - 2 * kind),
            in_diag_send.at[kind],
            in_diag_recv.at[kind],
            device(2 * kind - 1, 2 * kind - 1),
        )

    def back_lon(kind, band):
        return remote(
            context,
            kind,
            (band + 1 - kind, 2 - 2 * kind),
            (band + 1 - kind, 2 * kind),
            back_lon_send.at[kind, band],
            back_lon_recv.at[kind, band],
            device(0, 1 - 2 * kind),
        )

    def back_lat(kind, col):
        return remote(
            context,
            kind,
            (3 - 3 * kind, col + 1 - kind),
            (3 * kind, col + 1 - kind),
            back_lat_send.at[kind, col],
            back_lat_recv.at[kind, col],
            device(1 - 2 * kind, 0),
        )

    def back_diag(kind):
        return remote(
            context,
            kind,
            (3 - 3 * kind, 2 - 2 * kind),
            (3 * kind, 2 * kind),
            back_diag_send.at[kind],
            back_diag_recv.at[kind],
            device(1 - 2 * kind, 1 - 2 * kind),
        )

    barrier = pltpu.get_barrier_semaphore()
    for lat_step, lon_step in ((0, 1), (0, -1), (1, 0), (-1, 0), (1, 1), (-1, -1)):
        pl.semaphore_signal(
            barrier, inc=1, device_id=device(lat_step, lon_step), device_id_type=MESH
        )

    def prepare(kind, band):
        parts = []
        for half in range(2):
            x_copy(kind, half, band).wait()
            raw = x_raw[level_of(kind, half), band]
            scaled = norm(raw.astype(F32), ln1_gain[...], ln1_bias[...]).astype(BF16)
            parts.append(dot(split_ref[...], jnp.concatenate((raw, scaled), axis=1)))
        for col in range(2):
            rows = slice(col * HALF, (col + 1) * HALF)
            block = jnp.concatenate((parts[0][rows], parts[1][rows]), axis=0).astype(BF16)
            tokens[kind, band, col] = block[:, :WIDTH]
            normed[kind, band + kind, col + kind] = block[:, WIDTH:]

    def prepare_edge(kind, carry):
        prepare(kind, 2 * kind)
        return carry

    def prepare_rest(step, carry):
        kind, place = step % 2, 1 + step // 2
        band = place + kind * (2 - 2 * place)
        prepare(kind, band)
        in_lon(kind, band).start()
        return carry

    lax.fori_loop(0, 2, prepare_edge, 0)
    pl.semaphore_wait(barrier, 6)
    for kind in range(2):
        in_lon(kind, 2 * kind).start()
        in_diag(kind).start()
        in_lat(kind, 0).start()
        in_lat(kind, 1).start()
    lax.fori_loop(0, 4, prepare_rest, 0)

    def allow(step, carry):
        kind, band = step % 2, step // 2
        first = lat * 3 * WIN_LAT + (band - kind) * WIN_LAT + lats * 3 * WIN_LAT
        usable = jnp.zeros((UNIT, UNIT), F32)
        for slot in range(WIN_LAT):
            row = first + slot + jnp.where(slot < row_shift, WIN_LAT, 0)
            value = valid_ref[lax.rem(row, lats * 3 * WIN_LAT)].astype(F32)
            usable = jnp.where(pairs_ref[1] == slot, value, usable)
        seam = jnp.where(kind == 0, (lat == lats - 1) & (band == 2), (lat == 0) & (band == 0))
        shift = row_shift.astype(F32)
        query_side = jnp.where(pairs_ref[0] < shift, 1.0, 0.0)
        key_side = jnp.where(pairs_ref[1] < shift, 1.0, 0.0)
        apart = jnp.abs(query_side - key_side) * jnp.where(seam, 1.0, 0.0)
        apart = apart + (1.0 - pairs_ref[2]) * jnp.where(kind == 0, 0.0, 1.0)
        serves = (apart < 0.5) & (jnp.maximum(usable, pairs_ref[3]) > 0.5)
        bias[kind, band] = jnp.where(serves, 0.0, -jnp.inf)
        return carry

    lax.fori_loop(0, 6, allow, 0)
    weights[0].wait()

    row_bf, col_bf = row_shift.astype(F32).astype(BF16), col_shift.astype(F32).astype(BF16)

    def pick(ref, kind, band, col, below):
        low_i, low_j = slot_i_ref[...] < row_bf, slot_j_ref[...] < col_bf
        near, far = (1, 0) if below else (0, 1)
        top = jnp.where(low_j, ref[kind, band + near, col + near], ref[kind, band + near, col + far])
        bottom = jnp.where(low_j, ref[kind, band + far, col + near], ref[kind, band + far, col + far])
        return jnp.where(low_i, top, bottom)

    lane = lax.broadcasted_iota(jnp.int32, (UNIT, 128), 1)

    def attend(stage):
        def body(kind, carry):
            places = []
            for item in range(2):
                band, col = ((item, 0), (item, 1), (2, item))[stage]
                places.append((band + kind * (2 - 2 * band), col + kind * (1 - 2 * col)))
            window = jnp.concatenate(
                [pick(normed, kind, band, col, True) for band, col in places], axis=0
            )
            for part in range(3):
                columns = slice(part * WIDTH, (part + 1) * WIDTH)
                value = dot(window, w_qkv[:, columns])
                qkv[:, columns] = (value * 0.125 if part == 0 else value).astype(BF16)
            for item, (band, col) in enumerate(places):
                rows = slice(item * UNIT, (item + 1) * UNIT)
                for pair in range(4):
                    columns = slice(pair * 128, (pair + 1) * 128)
                    query = qkv[rows, columns].astype(F32)
                    query = jnp.concatenate(
                        (jnp.where(lane < 64, query, 0.0), jnp.where(lane < 64, 0.0, query)), axis=0
                    ).astype(BF16)
                    key = qkv[rows, WIDTH + pair * 128 : WIDTH + (pair + 1) * 128]
                    value = qkv[rows, 2 * WIDTH + pair * 128 : 2 * WIDTH + (pair + 1) * 128]
                    scores = lax.dot_general(
                        query, key, (((1,), (1,)), ((), ())), preferred_element_type=F32
                    )
                    mask = bias[kind, band]
                    scores = scores + jnp.concatenate((mask, mask), axis=0)
                    top = jnp.max(scores, axis=-1, keepdims=True)
                    share = jnp.exp(scores - top).astype(BF16)
                    value = jnp.concatenate((value, jnp.ones((UNIT, 128), BF16)), axis=1)
                    total = dot(share, value)
                    total = total[:, :128] / total[:, 128:]
                    context[kind, band + 1 - kind, col + 1 - kind, :, columns] = jnp.where(
                        lane < 64, total[:UNIT], total[UNIT:]
                    ).astype(BF16)
            return carry

        lax.fori_loop(0, 2, body, 0)

    attend(0)
    for kind in range(2):
        for band in range(3):
            in_lon(kind, band).wait_recv()
    attend(1)
    for kind in range(2):
        back_lon(kind, kind).start()
        back_lon(kind, 1 + kind).start()
    for kind in range(2):
        in_lat(kind, 0).wait_recv()
        in_lat(kind, 1).wait_recv()
        in_diag(kind).wait_recv()
    attend(2)
    for kind in range(2):
        back_lon(kind, 2 - 2 * kind).start()
        back_diag(kind).start()
        back_lat(kind, 0).start()
        back_lat(kind, 1).start()
    for copy in weights[1:4]:
        copy.wait()

    def finish(stage):
        def body(kind, carry):
            places = []
            for item in range(2):
                band, col = ((1 + item, 1), (1 + item, 0), (0, item))[stage]
                places.append((band + kind * (2 - 2 * band), col + kind * (1 - 2 * col)))
            attended = jnp.concatenate(
                [pick(context, kind, band, col, False) for band, col in places], axis=0
            )
            base = jnp.concatenate([tokens[kind, band, col] for band, col in places], axis=0)
            residual = base.astype(F32) + dot(attended, w_proj[...]) + b_proj[...]
            residual = residual.astype(BF16).astype(F32)
            scaled = norm(residual, ln2_gain[...], ln2_bias[...]).astype(BF16)
            total = residual + b_fc2[...]
            for part in range(4):
                columns = slice(part * WIDTH, (part + 1) * WIDTH)
                inner = dot(scaled, w_fc1[:, columns]) + b_fc1[:, columns]
                hidden = 0.5 * inner * (1.0 + lax.erf(inner * np.float32(0.5**0.5)))
                total = total + dot(hidden.astype(BF16), w_fc2[columns, :])
            total = total.astype(BF16).astype(F32)
            for item, (band, col) in enumerate(places):
                mixed[kind, band, col] = total[item * UNIT : (item + 1) * UNIT]
            return carry

        lax.fori_loop(0, 2, body, 0)

    finish(0)
    for kind in range(2):
        for band in range(3):
            back_lon(kind, band).wait_recv()
    finish(1)
    for kind in range(2):
        back_lat(kind, 0).wait_recv()
        back_lat(kind, 1).wait_recv()
        back_diag(kind).wait_recv()
    finish(2)

    def group(step, carry):
        kind, band = step % 2, step // 2
        for half in range(2):
            rows = slice(half * HALF, (half + 1) * HALF)
            level = jnp.concatenate((mixed[kind, band, 0, rows], mixed[kind, band, 1, rows]), axis=0)
            parts = dot(gather_ref[...], level.astype(BF16))
            parts = jnp.concatenate([parts[40 * part : 40 * part + 40] for part in range(4)], axis=1)
            grouped[step, half * 40 : half * 40 + 40] = norm(parts, merge_gain[...], merge_bias[...])
        return carry

    lax.fori_loop(0, 6, group, 0)
    weights[4].wait()
    for part in range(4):
        columns = slice(part * 256, (part + 1) * 256)
        merged = dot(
            grouped[...].reshape(480, FF).astype(BF16), w_merge[:, columns]
        )
        for step in range(6):
            kind, band = step % 2, step // 2
            for half in range(2):
                for row in range(3):
                    first = step * 80 + half * 40 + row * 12
                    out_ref[level_of(kind, half), band * 3 + row, :, columns] = merged[
                        first : first + 12
                    ].astype(BF16)

    for kind in range(2):
        for band in range(3):
            in_lon(kind, band).wait_send()
            back_lon(kind, band).wait_send()
        for col in range(2):
            in_lat(kind, col).wait_send()
            back_lat(kind, col).wait_send()
        in_diag(kind).wait_send()
        back_diag(kind).wait_send()


def solution(mesh):
    lats, lons = mesh.shape["lat"], mesh.shape["lon"]

    def on_device(
        tokens,
        lat_shift,
        lon_shift,
        lat_valid,
        ln1_gain,
        ln1_bias,
        w_qkv,
        w_proj,
        b_proj,
        ln2_gain,
        ln2_bias,
        w_fc1,
        b_fc1,
        w_fc2,
        b_fc2,
        merge_gain,
        merge_bias,
        w_merge,
    ):
        smem = pl.BlockSpec(memory_space=pltpu.SMEM)
        vmem = pl.BlockSpec(memory_space=pltpu.VMEM)
        hbm = pl.BlockSpec(memory_space=pl.ANY)
        dma = pltpu.SemaphoreType.DMA
        vectors = (
            ln1_gain,
            ln1_bias,
            b_proj,
            ln2_gain,
            ln2_bias,
            b_fc1,
            b_fc2,
            merge_gain,
            merge_bias,
        )
        return pl.pallas_call(
            functools.partial(block_kernel, lats, lons),
            out_shape=jax.ShapeDtypeStruct((4, 9, 12, 1024), BF16),
            in_specs=[smem] * 3 + [vmem] * 14 + [hbm] * 6,
            out_specs=vmem,
            scratch_shapes=[
                pltpu.VMEM((4, 3, UNIT, WIDTH), BF16),
                pltpu.VMEM((WIDTH, 3 * WIDTH), BF16),
                pltpu.VMEM((WIDTH, WIDTH), BF16),
                pltpu.VMEM((WIDTH, FF), BF16),
                pltpu.VMEM((FF, WIDTH), BF16),
                pltpu.VMEM((FF, 1024), BF16),
                pltpu.VMEM((2, 3, 2, UNIT, WIDTH), BF16),
                pltpu.VMEM((2, 4, 3, UNIT, WIDTH), BF16),
                pltpu.VMEM((2, 4, 3, UNIT, WIDTH), BF16),
                pltpu.VMEM((2, 3, 2, UNIT, WIDTH), F32),
                pltpu.VMEM((2, 3, UNIT, UNIT), F32),
                pltpu.VMEM((2 * UNIT, 3 * WIDTH), BF16),
                pltpu.VMEM((6, 80, FF), F32),
                dma((4, 3)),
                dma((5,)),
            ]
            + [dma((2, 3))] * 2
            + [dma((2, 2))] * 2
            + [dma((2,))] * 2
            + [dma((2, 3))] * 2
            + [dma((2, 2))] * 2
            + [dma((2,))] * 2,
            compiler_params=pltpu.CompilerParams(
                collective_id=0, has_side_effects=True, vmem_limit_bytes=58 * 1024 * 1024
            ),
        )(
            lat_shift,
            lon_shift,
            lat_valid,
            *constants(),
            *(vector.reshape(1, -1) for vector in vectors),
            tokens.reshape(4, 3, UNIT, WIDTH),
            w_qkv,
            w_proj,
            w_fc1,
            w_fc2,
            w_merge,
        )

    return jax.shard_map(
        on_device,
        mesh=mesh,
        in_specs=(P(None, "lat", "lon", None),) + (P(),) * 17,
        out_specs=P(None, "lat", "lon", None),
        check_vma=False,
    )
```

```python
import functools

import jax
import jax.numpy as jnp
import numpy as np
from jax import lax
from jax.experimental import pallas as pl
from jax.experimental.pallas import tpu as pltpu
from jax.sharding import PartitionSpec as P

WIN_LAT = 6
WIN_LON = 12
UNIT = 144
HALF = 72
WIDTH = 512
FF = 2048
NORM_EPS = 1e-05
MESH = pl.DeviceIdType.MESH
BF16 = jnp.bfloat16
F32 = jnp.float32


def constants():
    rows = np.arange(UNIT)
    block, within = rows // HALF, rows % HALF
    source = within // WIN_LON * 24 + block * WIN_LON + within % WIN_LON
    split = np.zeros((UNIT, UNIT), np.float32)
    split[rows, source] = 1.0
    gather = np.zeros((192, 192), np.float32)
    for part in range(4):
        col_odd, row_odd = part // 2, part % 2
        for col in range(12):
            for level in range(4):
                kind, half = (1, level // 3) if level in (0, 3) else (0, level - 1)
                token = kind * 96 + col // 6 * 48 + row_odd * 24 + half * 12 + 2 * (col % 6) + col_odd
                gather[part * 48 + col * 4 + level, token] = 1.0
    slot_i, slot_j = rows // 24, rows % WIN_LON
    half = rows // WIN_LON % 2
    wide = np.ones((1, WIDTH), np.float32)
    grid = np.ones((UNIT, UNIT), np.float32)
    pairs = np.stack(
        (
            slot_i[:, None] * grid,
            slot_i[None, :] * grid,
            (half[:, None] == half[None, :]) * grid,
            np.eye(UNIT),
        )
    )
    return (
        jnp.asarray(split, BF16),
        jnp.asarray(gather, BF16),
        jnp.asarray(slot_i[:, None] * wide, BF16),
        jnp.asarray(slot_j[:, None] * wide, BF16),
        jnp.asarray(pairs, F32),
    )


def norm(values, gain, bias):
    mean = jnp.mean(values, axis=-1, keepdims=True)
    centred = values - mean
    var = jnp.mean(centred * centred, axis=-1, keepdims=True)
    return centred * lax.rsqrt(var + NORM_EPS) * gain + bias


def dot(left, right):
    return jnp.dot(left, right, preferred_element_type=F32)


def block_kernel(
    lats,
    lons,
    row_shift,
    col_shift_ref,
    valid_ref,
    split_ref,
    gather_ref,
    slot_i_ref,
    slot_j_ref,
    pairs_ref,
    ln1_gain,
    ln1_bias,
    b_proj,
    ln2_gain,
    ln2_bias,
    b_fc1,
    b_fc2,
    merge_gain,
    merge_bias,
    x_hbm,
    w_qkv_hbm,
    w_proj_hbm,
    w_fc1_hbm,
    w_fc2_hbm,
    w_merge_hbm,
    out_ref,
    x_raw,
    w_qkv,
    w_proj,
    w_fc1,
    w_fc2,
    w_merge,
    tokens,
    normed,
    context,
    mixed,
    bias,
    qkv,
    grouped,
    x_sem,
    w_sem,
    in_lon_send,
    in_lon_recv,
    in_lat_send,
    in_lat_recv,
    in_diag_send,
    in_diag_recv,
    back_lon_send,
    back_lon_recv,
    back_lat_send,
    back_lat_recv,
    back_diag_send,
    back_diag_recv,
):
    lat, lon = lax.axis_index("lat"), lax.axis_index("lon")
    col_shift = col_shift_ref[0]
    side = 0 if row_shift <= 3 else 1
    count = {1: 32, 2: 48, 3: 80}[row_shift if side == 0 else WIN_LAT - row_shift]
    crossing = pl.ds(side * (UNIT - count), count)
    weights = [
        pltpu.make_async_copy(source, target, w_sem.at[place])
        for place, (source, target) in enumerate(
            (
                (w_qkv_hbm, w_qkv),
                (w_proj_hbm, w_proj),
                (w_fc1_hbm, w_fc1),
                (w_fc2_hbm, w_fc2),
                (w_merge_hbm, w_merge),
            )
        )
    ]

    def level_of(kind, half):
        return 1 + half + kind * (2 * half - 1)

    def x_copy(kind, half, band):
        level = level_of(kind, half)
        return pltpu.make_async_copy(
            x_hbm.at[level, band], x_raw.at[level, band], x_sem.at[level, band]
        )

    for band in range(3):
        for kind in range(2):
            for half in range(2):
                x_copy(kind, half, band).start()
    for copy in weights:
        copy.start()

    def device(lat_step, lon_step):
        return {
            "lat": lax.rem(lat + lat_step + lats, lats),
            "lon": lax.rem(lon + lon_step + lons, lons),
        }

    def remote(ref, kind, source, target, send, recv, place, rows=pl.ds(0, UNIT)):
        return pltpu.make_async_remote_copy(
            src_ref=ref.at[kind, source[0], source[1], rows],
            dst_ref=ref.at[kind, target[0], target[1], rows],
            send_sem=send,
            recv_sem=recv,
            device_id=place,
            device_id_type=MESH,
        )

    def in_lon(kind, band):
        return remote(
            normed,
            kind,
            (band + side, 2 * kind),
            (band + side, 2 - 2 * kind),
            in_lon_send.at[kind, band],
            in_lon_recv.at[kind, band],
            device(0, 2 * kind - 1),
        )

    def in_lat(kind, col):
        return remote(
            normed,
            kind,
            (3 * side, col + kind),
            (3 - 3 * side, col + kind),
            in_lat_send.at[kind, col],
            in_lat_recv.at[kind, col],
            device(2 * side - 1, 0),
            crossing,
        )

    def in_diag(kind):
        return remote(
            normed,
            kind,
            (3 * side, 2 * kind),
            (3 - 3 * side, 2 - 2 * kind),
            in_diag_send.at[kind],
            in_diag_recv.at[kind],
            device(2 * side - 1, 2 * kind - 1),
            crossing,
        )

    def back_lon(kind, band):
        return remote(
            context,
            kind,
            (band + 1 - side, 2 - 2 * kind),
            (band + 1 - side, 2 * kind),
            back_lon_send.at[kind, band],
            back_lon_recv.at[kind, band],
            device(0, 1 - 2 * kind),
        )

    def back_lat(kind, col):
        return remote(
            context,
            kind,
            (3 - 3 * side, col + 1 - kind),
            (3 * side, col + 1 - kind),
            back_lat_send.at[kind, col],
            back_lat_recv.at[kind, col],
            device(1 - 2 * side, 0),
            crossing,
        )

    def back_diag(kind):
        return remote(
            context,
            kind,
            (3 - 3 * side, 2 - 2 * kind),
            (3 * side, 2 * kind),
            back_diag_send.at[kind],
            back_diag_recv.at[kind],
            device(1 - 2 * side, 1 - 2 * kind),
            crossing,
        )

    neighbours = [(0, 1), (0, -1)] + [(a, b) for a in (1, -1) for b in (0, 1, -1)]
    barrier = pltpu.get_barrier_semaphore()
    for lat_step, lon_step in neighbours:
        pl.semaphore_signal(
            barrier, inc=1, device_id=device(lat_step, lon_step), device_id_type=MESH
        )

    def prepare(step, carry):
        kind, band = step % 2, step // 2
        raws, norms = [], []
        for half in range(2):
            x_copy(kind, half, band).wait()
            raw = x_raw[level_of(kind, half), band].astype(F32)
            raws.append(raw)
            norms.append(norm(raw, ln1_gain[...], ln1_bias[...]))
        parts = []
        for third in range(2):
            rows = [slice(24 * i, 24 * i + 24) for i in range(3 * third, 3 * third + 3)]
            mixed_rows = [
                jnp.concatenate([level[row] for row in rows for level in levels], axis=0)
                for levels in (raws, norms)
            ]
            parts.append(dot(split_ref[...], jnp.concatenate(mixed_rows, axis=1).astype(BF16)))
        for col in range(2):
            rows = slice(col * HALF, (col + 1) * HALF)
            block = jnp.concatenate((parts[0][rows], parts[1][rows]), axis=0).astype(BF16)
            tokens[kind, band, col] = block[:, :WIDTH]
            normed[kind, band + side, col + kind] = block[:, WIDTH:]

        @pl.when(step == 0)
        def _():
            pl.semaphore_wait(barrier, len(neighbours))

        in_lon(kind, band).start()
        return carry

    lax.fori_loop(0, 6, prepare, 0)
    for kind in range(2):
        in_diag(kind).start()
        in_lat(kind, 0).start()
        in_lat(kind, 1).start()

    def allow(step, carry):
        kind, band = step % 2, step // 2
        first = lat * 3 * WIN_LAT + (band - side) * WIN_LAT + lats * 3 * WIN_LAT
        usable = jnp.zeros((UNIT, UNIT), F32)
        for slot in range(WIN_LAT):
            row = first + slot + (WIN_LAT if slot < row_shift else 0)
            value = valid_ref[lax.rem(row, lats * 3 * WIN_LAT)].astype(F32)
            usable = jnp.where(pairs_ref[1] == slot, value, usable)
        seam = (lat == 0) & (band == 0) if side else (lat == lats - 1) & (band == 2)
        query_side = jnp.where(pairs_ref[0] < row_shift, 1.0, 0.0)
        key_side = jnp.where(pairs_ref[1] < row_shift, 1.0, 0.0)
        apart = jnp.abs(query_side - key_side) * jnp.where(seam, 1.0, 0.0)
        apart = apart + (1.0 - pairs_ref[2]) * jnp.where(kind == 0, 0.0, 1.0)
        serves = (apart < 0.5) & (jnp.maximum(usable, pairs_ref[3]) > 0.5)
        bias[kind, band] = jnp.where(serves, 0.0, -jnp.inf)
        return carry

    lax.fori_loop(0, 6, allow, 0)
    weights[0].wait()

    col_bf = col_shift.astype(F32).astype(BF16)

    def pick(ref, kind, band, col, below):
        low_i, low_j = slot_i_ref[...] < BF16(row_shift), slot_j_ref[...] < col_bf
        near, far = (1, 0) if below else (0, 1)
        top = jnp.where(low_j, ref[kind, band + near, col + near], ref[kind, band + near, col + far])
        bottom = jnp.where(low_j, ref[kind, band + far, col + near], ref[kind, band + far, col + far])
        return jnp.where(low_i, top, bottom)

    lane = lax.broadcasted_iota(jnp.int32, (UNIT, 128), 1)

    def places_of(kind, rows, cols):
        return [
            (2 - row if side else row, col + kind * (1 - 2 * col)) for row, col in zip(rows, cols)
        ]

    def attend(step, carry):
        kind, stage = step % 2, step // 2
        last = stage // 2

        @pl.when(stage == 1)
        def _():
            for band in range(3):
                in_lon(kind, band).wait_recv()

        @pl.when(stage == 2)
        def _():
            in_lat(kind, 0).wait_recv()
            in_lat(kind, 1).wait_recv()
            in_diag(kind).wait_recv()

        places = places_of(
            kind,
            [item + last * (2 - item) for item in range(2)],
            [stage * (1 - last) + last * item for item in range(2)],
        )
        window = jnp.concatenate(
            [pick(normed, kind, band, col, True) for band, col in places], axis=0
        )
        for part in range(3):
            columns = slice(part * WIDTH, (part + 1) * WIDTH)
            value = dot(window, w_qkv[:, columns])
            qkv[:, columns] = (value * 0.125 if part == 0 else value).astype(BF16)
        for item, (band, col) in enumerate(places):
            rows = slice(item * UNIT, (item + 1) * UNIT)
            for pair in range(4):
                columns = slice(pair * 128, (pair + 1) * 128)
                query = qkv[rows, columns].astype(F32)
                query = jnp.concatenate(
                    (jnp.where(lane < 64, query, 0.0), jnp.where(lane < 64, 0.0, query)), axis=0
                ).astype(BF16)
                key = qkv[rows, WIDTH + pair * 128 : WIDTH + (pair + 1) * 128]
                value = qkv[rows, 2 * WIDTH + pair * 128 : 2 * WIDTH + (pair + 1) * 128]
                scores = lax.dot_general(
                    query, key, (((1,), (1,)), ((), ())), preferred_element_type=F32
                )
                mask = bias[kind, band]
                scores = scores + jnp.concatenate((mask, mask), axis=0)
                top = jnp.max(scores, axis=-1, keepdims=True)
                share = jnp.exp(scores - top).astype(BF16)
                value = jnp.concatenate((value, jnp.ones((UNIT, 128), BF16)), axis=1)
                total = dot(share, value)
                total = total[:, :128] / total[:, 128:]
                context[kind, band + 1 - side, col + 1 - kind, :, columns] = jnp.where(
                    lane < 64, total[:UNIT], total[UNIT:]
                ).astype(BF16)

        @pl.when(stage == 1)
        def _():
            for band, _ in places:
                back_lon(kind, band).start()

        @pl.when(stage == 2)
        def _():
            back_lon(kind, 2 - 2 * side).start()
            back_diag(kind).start()
            back_lat(kind, 0).start()
            back_lat(kind, 1).start()

        return carry

    lax.fori_loop(0, 6, attend, 0)
    for copy in weights[1:4]:
        copy.wait()

    def finish(step, carry):
        kind, stage = step % 2, step // 2
        last = stage // 2

        @pl.when(stage == 1)
        def _():
            for band in range(3):
                back_lon(kind, band).wait_recv()

        @pl.when(stage == 2)
        def _():
            back_lat(kind, 0).wait_recv()
            back_lat(kind, 1).wait_recv()
            back_diag(kind).wait_recv()

        places = places_of(
            kind,
            [(1 + item) * (1 - last) for item in range(2)],
            [(1 - stage) * (1 - last) + last * item for item in range(2)],
        )
        attended = jnp.concatenate(
            [pick(context, kind, band, col, False) for band, col in places], axis=0
        )
        base = jnp.concatenate([tokens[kind, band, col] for band, col in places], axis=0)
        residual = base.astype(F32) + dot(attended, w_proj[...]) + b_proj[...]
        residual = residual.astype(BF16).astype(F32)
        scaled = norm(residual, ln2_gain[...], ln2_bias[...]).astype(BF16)
        total = residual + b_fc2[...]
        for part in range(4):
            columns = slice(part * WIDTH, (part + 1) * WIDTH)
            inner = dot(scaled, w_fc1[:, columns]) + b_fc1[:, columns]
            hidden = 0.5 * inner * (1.0 + lax.erf(inner * np.float32(0.5**0.5)))
            total = total + dot(hidden.astype(BF16), w_fc2[columns, :])
        total = total.astype(BF16).astype(F32)
        for item, (band, col) in enumerate(places):
            mixed[kind, band, col] = total[item * UNIT : (item + 1) * UNIT]
        return carry

    lax.fori_loop(0, 6, finish, 0)

    def group(step, carry):
        band = step // 3
        rows = pl.ds(pl.multiple_of(step % 3 * 48, 48), 48)
        level = [mixed[kind, band, col, rows] for kind in range(2) for col in range(2)]
        parts = dot(gather_ref[...], jnp.concatenate(level, axis=0).astype(BF16))
        parts = jnp.concatenate([parts[48 * part : 48 * part + 48] for part in range(4)], axis=1)
        grouped[step] = norm(parts, merge_gain[...], merge_bias[...]).astype(BF16)
        return carry

    lax.fori_loop(0, 9, group, 0)
    weights[4].wait()
    for part in range(4):
        columns = slice(part * 256, (part + 1) * 256)
        merged = dot(grouped[...].reshape(432, FF), w_merge[:, columns])
        out_ref[:, columns] = merged.astype(BF16)

    for kind in range(2):
        for band in range(3):
            in_lon(kind, band).wait_send()
            back_lon(kind, band).wait_send()
        for col in range(2):
            in_lat(kind, col).wait_send()
            back_lat(kind, col).wait_send()
        in_diag(kind).wait_send()
        back_diag(kind).wait_send()


def solution(mesh):
    lats, lons = mesh.shape["lat"], mesh.shape["lon"]

    def on_device(
        tokens,
        lat_shift,
        lon_shift,
        lat_valid,
        ln1_gain,
        ln1_bias,
        w_qkv,
        w_proj,
        b_proj,
        ln2_gain,
        ln2_bias,
        w_fc1,
        b_fc1,
        w_fc2,
        b_fc2,
        merge_gain,
        merge_bias,
        w_merge,
    ):
        smem = pl.BlockSpec(memory_space=pltpu.SMEM)
        vmem = pl.BlockSpec(memory_space=pltpu.VMEM)
        hbm = pl.BlockSpec(memory_space=pl.ANY)
        dma = pltpu.SemaphoreType.DMA
        vectors = (
            ln1_gain,
            ln1_bias,
            b_proj,
            ln2_gain,
            ln2_bias,
            b_fc1,
            b_fc2,
            merge_gain,
            merge_bias,
        )
        def variant(row_shift, *operands):
            return pl.pallas_call(
                functools.partial(block_kernel, lats, lons, row_shift),
                out_shape=jax.ShapeDtypeStruct((432, 1024), BF16),
                in_specs=[smem] * 2 + [vmem] * 14 + [hbm] * 6,
                out_specs=vmem,
                scratch_shapes=[
                    pltpu.VMEM((4, 3, UNIT, WIDTH), BF16),
                    pltpu.VMEM((WIDTH, 3 * WIDTH), BF16),
                    pltpu.VMEM((WIDTH, WIDTH), BF16),
                    pltpu.VMEM((WIDTH, FF), BF16),
                    pltpu.VMEM((FF, WIDTH), BF16),
                    pltpu.VMEM((FF, 1024), BF16),
                    pltpu.VMEM((2, 3, 2, UNIT, WIDTH), BF16),
                    pltpu.VMEM((2, 4, 3, UNIT, WIDTH), BF16),
                    pltpu.VMEM((2, 4, 3, UNIT, WIDTH), BF16),
                    pltpu.VMEM((2, 3, 2, UNIT, WIDTH), F32),
                    pltpu.VMEM((2, 3, UNIT, UNIT), F32),
                    pltpu.VMEM((2 * UNIT, 3 * WIDTH), BF16),
                    pltpu.VMEM((9, 48, FF), BF16),
                    dma((4, 3)),
                    dma((5,)),
                ]
                + [dma((2, 3))] * 2
                + [dma((2, 2))] * 2
                + [dma((2,))] * 2
                + [dma((2, 3))] * 2
                + [dma((2, 2))] * 2
                + [dma((2,))] * 2,
                compiler_params=pltpu.CompilerParams(
                    collective_id=row_shift, has_side_effects=True, vmem_limit_bytes=58 * 1024 * 1024
                ),
            )(*operands)

        merged = lax.switch(
            lat_shift[0] - 1,
            [functools.partial(variant, row_shift) for row_shift in range(1, WIN_LAT)],
            lon_shift,
            lat_valid,
            *constants(),
            *(vector.reshape(1, -1) for vector in vectors),
            tokens.reshape(4, 3, UNIT, WIDTH),
            w_qkv,
            w_proj,
            w_fc1,
            w_fc2,
            w_merge,
        )
        return merged.reshape(9, 12, 4, 1024).transpose(2, 0, 1, 3)

    return jax.shard_map(
        on_device,
        mesh=mesh,
        in_specs=(P(None, "lat", "lon", None),) + (P(),) * 17,
        out_specs=P(None, "lat", "lon", None),
        check_vma=False,
    )
```

```python
import functools

import jax
import jax.numpy as jnp
import numpy as np
from jax import lax
from jax.experimental import pallas as pl
from jax.experimental.pallas import tpu as pltpu
from jax.sharding import PartitionSpec as P

WIN_LAT = 6
WIN_LON = 12
UNIT = 144
HALF = 72
ROOM = 80
WIDTH = 512
FF = 2048
NORM_EPS = 1e-05
MESH = pl.DeviceIdType.MESH
BF16 = jnp.bfloat16
F32 = jnp.float32


def column_split(count):
    matrix = np.zeros((24 * count, 24 * count), np.float32)
    for row in range(count):
        for col in range(24):
            matrix[col // 6 * 6 * count + row * 6 + col % 6, row * 24 + col] = 1.0
    return jnp.asarray(matrix, BF16)


def constants():
    gather = np.zeros((192, 192), np.float32)
    for part in range(4):
        col_odd, row_odd = part // 2, part % 2
        for col in range(12):
            for level in range(4):
                kind, half = (1, level // 3) if level in (0, 3) else (0, level - 1)
                block, slot = col // 6, 2 * (col % 6) + col_odd
                token = kind * 96 + block * 48 + slot // 6 * 24 + row_odd * 12 + half * 6 + slot % 6
                gather[part * 48 + col * 4 + level, token] = 1.0
    rows = np.arange(UNIT)
    slot_i = rows % HALF // WIN_LON
    half = rows // 6 % 2
    grid = np.ones((UNIT, UNIT), np.float32)
    pairs = np.stack(
        (
            slot_i[:, None] * grid,
            slot_i[None, :] * grid,
            (half[:, None] == half[None, :]) * grid,
            np.eye(UNIT),
        )
    )
    slot_j = (rows[:HALF, None] % 6) * np.ones((1, WIDTH))
    return (
        column_split(8),
        column_split(4),
        jnp.asarray(gather, BF16),
        jnp.asarray(slot_j, F32),
        jnp.asarray(pairs, F32),
    )


def norm(values, gain, bias):
    mean = jnp.mean(values, axis=-1, keepdims=True)
    centred = values - mean
    var = jnp.mean(centred * centred, axis=-1, keepdims=True)
    return centred * lax.rsqrt(var + NORM_EPS) * gain + bias


def dot(left, right):
    return jnp.dot(left, right, preferred_element_type=F32)


def block_kernel(
    lats,
    lons,
    row_shift,
    turn,
    col_shift_ref,
    valid_ref,
    split8_ref,
    split4_ref,
    gather_ref,
    slot_j_ref,
    pairs_ref,
    ln1_gain,
    ln1_bias,
    b_proj,
    ln2_gain,
    ln2_bias,
    b_fc1,
    b_fc2,
    merge_gain,
    merge_bias,
    x_hbm,
    w_qkv_hbm,
    w_proj_hbm,
    w_fc1_hbm,
    w_fc2_hbm,
    w_merge_hbm,
    out_ref,
    x_raw,
    w_qkv,
    w_proj,
    w_fc1,
    w_fc2,
    w_merge,
    tokens,
    normed,
    context,
    mixed,
    bias,
    qkv,
    hidden,
    grouped,
    x_sem,
    w_sem,
    in_lon_send,
    in_lon_recv,
    in_lat_send,
    in_lat_recv,
    in_diag_send,
    in_diag_recv,
    back_lon_send,
    back_lon_recv,
    back_lat_send,
    back_lat_recv,
    back_diag_send,
    back_diag_recv,
):
    lat, lon = lax.axis_index("lat"), lax.axis_index("lon")
    col_shift = col_shift_ref[0]
    side = 0 if row_shift <= 3 else 1
    crossing = pl.ds(48, 32) if side else pl.ds(0, 16 * row_shift)
    whole = pl.ds(0, ROOM)
    weights = [
        pltpu.make_async_copy(source, target, w_sem.at[place])
        for place, (source, target) in enumerate(
            (
                (w_qkv_hbm, w_qkv),
                (w_proj_hbm, w_proj),
                (w_fc1_hbm, w_fc1),
                (w_fc2_hbm, w_fc2),
                (w_merge_hbm, w_merge),
            )
        )
    ]

    def level_of(kind, half):
        return 1 + half + kind * (2 * half - 1)

    def x_copy(kind, half, band):
        level = level_of(kind, half)
        return pltpu.make_async_copy(
            x_hbm.at[level, band], x_raw.at[level, band], x_sem.at[level, band]
        )

    for band in range(3):
        for kind in range(2):
            for half in range(2):
                x_copy(kind, half, band).start()
    for copy in weights:
        copy.start()

    def device(lat_step, lon_step):
        return {
            "lat": lax.rem(lat + lat_step + lats, lats),
            "lon": lax.rem(lon + lon_step + lons, lons),
        }

    def remote(ref, source, target, send, recv, place):
        return pltpu.make_async_remote_copy(
            src_ref=ref.at[source],
            dst_ref=ref.at[target],
            send_sem=send,
            recv_sem=recv,
            device_id=place,
            device_id_type=MESH,
        )

    both = slice(None)

    def in_lon(kind, band):
        return remote(
            normed,
            (kind, band + side, 2 * turn, turn, whole),
            (kind, band + side, 2 - 2 * turn, turn, whole),
            in_lon_send.at[kind, band],
            in_lon_recv.at[kind, band],
            device(0, 2 * turn - 1),
        )

    def in_lat(kind, col):
        return remote(
            normed,
            (kind, 3 * side, col + turn, both, crossing),
            (kind, 3 - 3 * side, col + turn, both, crossing),
            in_lat_send.at[kind, col],
            in_lat_recv.at[kind, col],
            device(2 * side - 1, 0),
        )

    def in_diag(kind):
        return remote(
            normed,
            (kind, 3 * side, 2 * turn, turn, crossing),
            (kind, 3 - 3 * side, 2 - 2 * turn, turn, crossing),
            in_diag_send.at[kind],
            in_diag_recv.at[kind],
            device(2 * side - 1, 2 * turn - 1),
        )

    def back_lon(kind, band):
        return remote(
            context,
            (kind, band + 1 - side, 2 - 2 * turn, turn, whole),
            (kind, band + 1 - side, 2 * turn, turn, whole),
            back_lon_send.at[kind, band],
            back_lon_recv.at[kind, band],
            device(0, 1 - 2 * turn),
        )

    def back_lat(kind, col):
        return remote(
            context,
            (kind, 3 - 3 * side, col + 1 - turn, both, crossing),
            (kind, 3 * side, col + 1 - turn, both, crossing),
            back_lat_send.at[kind, col],
            back_lat_recv.at[kind, col],
            device(1 - 2 * side, 0),
        )

    def back_diag(kind):
        return remote(
            context,
            (kind, 3 - 3 * side, 2 - 2 * turn, turn, crossing),
            (kind, 3 * side, 2 * turn, turn, crossing),
            back_diag_send.at[kind],
            back_diag_recv.at[kind],
            device(1 - 2 * side, 1 - 2 * turn),
        )

    corner = 1 if side == turn else -1
    neighbours = [(0, 1), (0, -1), (1, 0), (-1, 0), (1, corner), (-1, -corner)]
    barrier = pltpu.get_barrier_semaphore()
    for lat_step, lon_step in neighbours:
        pl.semaphore_signal(
            barrier, inc=1, device_id=device(lat_step, lon_step), device_id_type=MESH
        )

    def prepare(kind, band):
        raws, norms = [], []
        for half in range(2):
            x_copy(kind, half, band).wait()
            raw = x_raw[level_of(kind, half), band].astype(F32)
            raws.append(raw)
            norms.append(norm(raw, ln1_gain[...], ln1_bias[...]))
        parts = []
        for matrix, places in ((split8_ref, range(4)), (split4_ref, range(4, 6))):
            rows = [slice(24 * i, 24 * i + 24) for i in places]
            mixed_rows = [
                jnp.concatenate([level[row] for row in rows for level in levels], axis=0)
                for levels in (raws, norms)
            ]
            parts.append(dot(matrix[...], jnp.concatenate(mixed_rows, axis=1).astype(BF16)))
        for col in range(2):
            halves = []
            for half in range(2):
                place = 2 * col + half
                halves.append(
                    jnp.concatenate(
                        (parts[0][48 * place : 48 * place + 48], parts[1][24 * place : 24 * place + 24]),
                        axis=0,
                    )
                )
                normed[kind, band + side, col + turn, half, :HALF] = halves[half][:, WIDTH:].astype(BF16)
            block = jnp.concatenate([half[:, :WIDTH] for half in halves], axis=0)
            tokens[kind, band, col] = block.astype(BF16)

    def prepare_band(band, carry):
        for kind in range(2):
            prepare(kind, band)

        @pl.when(band == 0)
        def _():
            pl.semaphore_wait(barrier, len(neighbours))

        for kind in range(2):
            in_lon(kind, band).start()
        return carry

    lax.fori_loop(0, 3, prepare_band, 0)
    for kind in range(2):
        in_diag(kind).start()
        in_lat(kind, 0).start()
        in_lat(kind, 1).start()

    def allow(band, carry):
        first = lat * 3 * WIN_LAT + (band - side) * WIN_LAT + lats * 3 * WIN_LAT
        usable = jnp.zeros((UNIT, UNIT), F32)
        for slot in range(WIN_LAT):
            row = first + slot + (WIN_LAT if slot < row_shift else 0)
            value = valid_ref[lax.rem(row, lats * 3 * WIN_LAT)].astype(F32)
            usable = jnp.where(pairs_ref[1] == slot, value, usable)
        seam = (lat == 0) & (band == 0) if side else (lat == lats - 1) & (band == 2)
        query_side = jnp.where(pairs_ref[0] < row_shift, 1.0, 0.0)
        key_side = jnp.where(pairs_ref[1] < row_shift, 1.0, 0.0)
        apart = jnp.abs(query_side - key_side) * jnp.where(seam, 1.0, 0.0)
        for kind in range(2):
            serves = (apart < 0.5) & (jnp.maximum(usable, pairs_ref[3]) > 0.5)
            if kind == 1:
                serves = serves & (pairs_ref[2] > 0.5)
            bias[kind, band] = jnp.where(serves, 0.0, -jnp.inf)
        return carry

    lax.fori_loop(0, 3, allow, 0)
    weights[0].wait()

    col_edge = col_shift.astype(F32)

    def pick(ref, kind, band, col, below):
        near, far = (1, 0) if below else (0, 1)
        low_i = lax.broadcasted_iota(jnp.int32, (HALF, WIDTH), 0) < WIN_LON * row_shift
        halves = []
        for half in range(2):

            def across(row):
                low, high = (
                    ref[kind, band + row, col + step, half, :HALF].astype(F32) for step in (near, far)
                )
                if half != turn:
                    return low if turn else high
                return jnp.where(slot_j_ref[...] + 6 * half < col_edge, low, high)

            halves.append(jnp.where(low_i, across(near), across(far)))
        return jnp.concatenate(halves, axis=0).astype(BF16)

    lane = lax.broadcasted_iota(jnp.int32, (UNIT, 128), 1)

    def places_of(rows, cols):
        return [
            (kind, 2 - row if side else row, 1 - col if turn else col)
            for kind in range(2)
            for row, col in zip(rows, cols)
        ]

    def attend_pair(place, item, pair):
        kind, band, col = place
        rows = pl.ds(item * UNIT, UNIT)
        columns = slice(pair * 128, (pair + 1) * 128)
        query = qkv[rows, columns].astype(F32)
        query = jnp.concatenate(
            (jnp.where(lane < 64, query, 0.0), jnp.where(lane < 64, 0.0, query)), axis=0
        ).astype(BF16)
        key = qkv[rows, WIDTH + pair * 128 : WIDTH + (pair + 1) * 128]
        value = qkv[rows, 2 * WIDTH + pair * 128 : 2 * WIDTH + (pair + 1) * 128]
        scores = lax.dot_general(query, key, (((1,), (1,)), ((), ())), preferred_element_type=F32)
        mask = bias[kind, band]
        scores = scores + jnp.concatenate((mask, mask), axis=0)
        top = jnp.max(scores, axis=-1, keepdims=True)
        share = jnp.exp(scores - top).astype(BF16)
        value = jnp.concatenate((value, jnp.ones((UNIT, 128), BF16)), axis=1)
        total = dot(share, value)
        total = total[:, :128] / total[:, 128:]
        total = jnp.where(lane < 64, total[:UNIT], total[UNIT:])
        for half in range(2):
            context[kind, band + 1 - side, col + 1 - turn, half, :HALF, columns] = total[
                half * HALF : (half + 1) * HALF
            ].astype(BF16)

    def attend(stage, carry):
        last = stage // 2

        @pl.when(stage == 1)
        def _():
            for kind in range(2):
                for band in range(3):
                    in_lon(kind, band).wait_recv()

        @pl.when(stage == 2)
        def _():
            for kind in range(2):
                in_lat(kind, 0).wait_recv()
                in_lat(kind, 1).wait_recv()
                in_diag(kind).wait_recv()

        places = places_of(
            [item + last * (2 - item) for item in range(2)],
            [stage * (1 - last) + last * item for item in range(2)],
        )
        window = jnp.concatenate([pick(normed, *place, True) for place in places], axis=0)
        for part in range(3):
            columns = slice(part * WIDTH, (part + 1) * WIDTH)
            value = dot(window, w_qkv[:, columns])
            qkv[:, columns] = (value * 0.125 if part == 0 else value).astype(BF16)
        for item, place in enumerate(places):
            for pair in range(4):
                attend_pair(place, item, pair)

        @pl.when(stage == 1)
        def _():
            for kind, band, _ in places:
                back_lon(kind, band).start()

        @pl.when(stage == 2)
        def _():
            for kind in range(2):
                back_lon(kind, 2 - 2 * side).start()
                back_diag(kind).start()
                back_lat(kind, 0).start()
                back_lat(kind, 1).start()

        return carry

    lax.fori_loop(0, 3, attend, 0)
    for copy in weights[1:4]:
        copy.wait()

    def finish(stage, carry):
        last = stage // 2

        @pl.when(stage == 1)
        def _():
            for kind in range(2):
                for band in range(3):
                    back_lon(kind, band).wait_recv()

        @pl.when(stage == 2)
        def _():
            for kind in range(2):
                back_lat(kind, 0).wait_recv()
                back_lat(kind, 1).wait_recv()
                back_diag(kind).wait_recv()

        places = places_of(
            [(1 + item) * (1 - last) for item in range(2)],
            [(1 - stage) * (1 - last) + last * item for item in range(2)],
        )
        attended = jnp.concatenate([pick(context, *place, False) for place in places], axis=0)
        base = jnp.concatenate([tokens[place] for place in places], axis=0)
        residual = base.astype(F32) + dot(attended, w_proj[...]) + b_proj[...]
        residual = residual.astype(BF16).astype(F32)
        scaled = norm(residual, ln2_gain[...], ln2_bias[...]).astype(BF16)
        for part in range(4):
            columns = slice(part * WIDTH, (part + 1) * WIDTH)
            inner = dot(scaled, w_fc1[:, columns]) + b_fc1[:, columns]
            gelu = 0.5 * inner * (1.0 + lax.erf(inner * np.float32(0.5**0.5)))
            hidden[:, columns] = gelu.astype(BF16)
        total = residual + b_fc2[...] + dot(hidden[...], w_fc2[...])
        total = total.astype(BF16).astype(F32)
        for item, place in enumerate(places):
            mixed[place] = total[item * UNIT : (item + 1) * UNIT]
        return carry

    lax.fori_loop(0, 3, finish, 0)

    def group(band, carry):
        for row in range(3):
            rows = [slice(half * HALF + row * 24, half * HALF + row * 24 + 24) for half in range(2)]
            level = [
                mixed[kind, band, col, part] for kind in range(2) for col in range(2) for part in rows
            ]
            parts = dot(gather_ref[...], jnp.concatenate(level, axis=0).astype(BF16))
            parts = jnp.concatenate([parts[48 * part : 48 * part + 48] for part in range(4)], axis=1)
            grouped[3 * band + row] = norm(parts, merge_gain[...], merge_bias[...]).astype(BF16)
        return carry

    lax.fori_loop(0, 3, group, 0)
    weights[4].wait()
    for part in range(4):
        columns = slice(part * 256, (part + 1) * 256)
        merged = dot(grouped[...].reshape(432, FF), w_merge[:, columns])
        out_ref[:, columns] = merged.astype(BF16)

    for kind in range(2):
        for band in range(3):
            in_lon(kind, band).wait_send()
            back_lon(kind, band).wait_send()
        for col in range(2):
            in_lat(kind, col).wait_send()
            back_lat(kind, col).wait_send()
        in_diag(kind).wait_send()
        back_diag(kind).wait_send()


def solution(mesh):
    lats, lons = mesh.shape["lat"], mesh.shape["lon"]

    def on_device(
        tokens,
        lat_shift,
        lon_shift,
        lat_valid,
        ln1_gain,
        ln1_bias,
        w_qkv,
        w_proj,
        b_proj,
        ln2_gain,
        ln2_bias,
        w_fc1,
        b_fc1,
        w_fc2,
        b_fc2,
        merge_gain,
        merge_bias,
        w_merge,
    ):
        smem = pl.BlockSpec(memory_space=pltpu.SMEM)
        vmem = pl.BlockSpec(memory_space=pltpu.VMEM)
        hbm = pl.BlockSpec(memory_space=pl.ANY)
        dma = pltpu.SemaphoreType.DMA
        vectors = (
            ln1_gain,
            ln1_bias,
            b_proj,
            ln2_gain,
            ln2_bias,
            b_fc1,
            b_fc2,
            merge_gain,
            merge_bias,
        )
        def variant(row_shift, turn, *operands):
            return pl.pallas_call(
                functools.partial(block_kernel, lats, lons, row_shift, turn),
                out_shape=jax.ShapeDtypeStruct((432, 1024), BF16),
                in_specs=[smem] * 2 + [vmem] * 14 + [hbm] * 6,
                out_specs=vmem,
                scratch_shapes=[
                    pltpu.VMEM((4, 3, UNIT, WIDTH), BF16),
                    pltpu.VMEM((WIDTH, 3 * WIDTH), BF16),
                    pltpu.VMEM((WIDTH, WIDTH), BF16),
                    pltpu.VMEM((WIDTH, FF), BF16),
                    pltpu.VMEM((FF, WIDTH), BF16),
                    pltpu.VMEM((FF, 1024), BF16),
                    pltpu.VMEM((2, 3, 2, UNIT, WIDTH), BF16),
                    pltpu.VMEM((2, 4, 3, 2, ROOM, WIDTH), BF16),
                    pltpu.VMEM((2, 4, 3, 2, ROOM, WIDTH), BF16),
                    pltpu.VMEM((2, 3, 2, UNIT, WIDTH), F32),
                    pltpu.VMEM((2, 3, UNIT, UNIT), F32),
                    pltpu.VMEM((4 * UNIT, 3 * WIDTH), BF16),
                    pltpu.VMEM((4 * UNIT, FF), BF16),
                    pltpu.VMEM((9, 48, FF), BF16),
                    dma((4, 3)),
                    dma((5,)),
                ]
                + [dma((2, 3))] * 2
                + [dma((2, 2))] * 2
                + [dma((2,))] * 2
                + [dma((2, 3))] * 2
                + [dma((2, 2))] * 2
                + [dma((2,))] * 2,
                compiler_params=pltpu.CompilerParams(
                    collective_id=row_shift + 5 * turn, has_side_effects=True, vmem_limit_bytes=58 * 1024 * 1024
                ),
            )(*operands)

        merged = lax.switch(
            lat_shift[0] - 1 + jnp.where(lon_shift[0] > 6, 5, 0),
            [
                functools.partial(variant, row_shift, turn)
                for turn in range(2)
                for row_shift in range(1, WIN_LAT)
            ],
            lon_shift,
            lat_valid,
            *constants(),
            *(vector.reshape(1, -1) for vector in vectors),
            tokens.reshape(4, 3, UNIT, WIDTH),
            w_qkv,
            w_proj,
            w_fc1,
            w_fc2,
            w_merge,
        )
        return merged.reshape(9, 12, 4, 1024).transpose(2, 0, 1, 3)

    return jax.shard_map(
        on_device,
        mesh=mesh,
        in_specs=(P(None, "lat", "lon", None),) + (P(),) * 17,
        out_specs=P(None, "lat", "lon", None),
        check_vma=False,
    )
```

```python
import functools

import jax
import jax.numpy as jnp
import numpy as np
from jax import lax
from jax.experimental import pallas as pl
from jax.experimental.pallas import tpu as pltpu
from jax.sharding import PartitionSpec as P

WIN_LAT = 6
WIN_LON = 12
UNIT = 144
HALF = 72
ROOM = 80
WIDTH = 512
FF = 2048
NORM_EPS = 1e-05
MESH = pl.DeviceIdType.MESH
BF16 = jnp.bfloat16
F32 = jnp.float32


def column_split(count):
    matrix = np.zeros((24 * count, 24 * count), np.float32)
    for row in range(count):
        for col in range(24):
            matrix[col // 6 * 6 * count + row * 6 + col % 6, row * 24 + col] = 1.0
    return jnp.asarray(matrix, BF16)


def constants():
    gather = np.zeros((192, 192), np.float32)
    for part in range(4):
        col_odd, row_odd = part // 2, part % 2
        for col in range(12):
            for level in range(4):
                kind, half = (1, level // 3) if level in (0, 3) else (0, level - 1)
                block, slot = col // 6, 2 * (col % 6) + col_odd
                token = kind * 96 + block * 48 + slot // 6 * 24 + row_odd * 12 + half * 6 + slot % 6
                gather[part * 48 + col * 4 + level, token] = 1.0
    rows = np.arange(UNIT)
    slot_i = rows % HALF // WIN_LON
    half = rows // 6 % 2
    grid = np.ones((UNIT, UNIT), np.float32)
    pairs = np.stack(
        (
            slot_i[:, None] * grid,
            slot_i[None, :] * grid,
            (half[:, None] == half[None, :]) * grid,
            np.eye(UNIT),
        )
    )
    slot_j = (rows[:HALF, None] % 6) * np.ones((1, WIDTH))
    return (
        column_split(8),
        column_split(4),
        jnp.asarray(gather, BF16),
        jnp.asarray(slot_j, F32),
        jnp.asarray(pairs, F32),
    )


def norm(values, gain, bias):
    mean = jnp.mean(values, axis=-1, keepdims=True)
    centred = values - mean
    var = jnp.mean(centred * centred, axis=-1, keepdims=True)
    return centred * lax.rsqrt(var + NORM_EPS) * gain + bias


def dot(left, right):
    return jnp.dot(left, right, preferred_element_type=F32)


def block_kernel(
    lats,
    lons,
    side,
    turn,
    row_shift_ref,
    col_shift_ref,
    valid_ref,
    split8_ref,
    split4_ref,
    gather_ref,
    slot_j_ref,
    pairs_ref,
    ln1_gain,
    ln1_bias,
    b_proj,
    ln2_gain,
    ln2_bias,
    b_fc1,
    b_fc2,
    merge_gain,
    merge_bias,
    x_hbm,
    w_qkv_hbm,
    w_proj_hbm,
    w_fc1_hbm,
    w_fc2_hbm,
    w_merge_hbm,
    out_ref,
    x_raw,
    w_qkv,
    w_proj,
    w_fc1,
    w_fc2,
    w_merge,
    tokens,
    normed,
    context,
    mixed,
    bias,
    qkv,
    hidden,
    grouped,
    x_sem,
    w_sem,
    in_lon_send,
    in_lon_recv,
    in_lat_send,
    in_lat_recv,
    in_diag_send,
    in_diag_recv,
    back_lon_send,
    back_lon_recv,
    back_lat_send,
    back_lat_recv,
    back_diag_send,
    back_diag_recv,
):
    lat, lon = lax.axis_index("lat"), lax.axis_index("lon")
    row_shift, col_shift = row_shift_ref[0], col_shift_ref[0]
    crossing = pl.ds(48, 32) if side else pl.ds(0, 48)
    whole = pl.ds(0, ROOM)
    weights = [
        pltpu.make_async_copy(source, target, w_sem.at[place])
        for place, (source, target) in enumerate(
            (
                (w_qkv_hbm, w_qkv),
                (w_proj_hbm, w_proj),
                (w_fc1_hbm, w_fc1),
                (w_fc2_hbm, w_fc2),
                (w_merge_hbm, w_merge),
            )
        )
    ]

    def level_of(kind, half):
        return 1 + half + kind * (2 * half - 1)

    def x_copy(kind, half, band):
        level = level_of(kind, half)
        return pltpu.make_async_copy(
            x_hbm.at[level, band], x_raw.at[level, band], x_sem.at[level, band]
        )

    for band in range(3):
        for kind in range(2):
            for half in range(2):
                x_copy(kind, half, band).start()
    for copy in weights:
        copy.start()

    def device(lat_step, lon_step):
        return {
            "lat": lax.rem(lat + lat_step + lats, lats),
            "lon": lax.rem(lon + lon_step + lons, lons),
        }

    def remote(ref, source, target, send, recv, place):
        return pltpu.make_async_remote_copy(
            src_ref=ref.at[source],
            dst_ref=ref.at[target],
            send_sem=send,
            recv_sem=recv,
            device_id=place,
            device_id_type=MESH,
        )

    both = slice(None)

    def in_lon(kind, band):
        return remote(
            normed,
            (kind, band + side, 2 * turn, turn, whole),
            (kind, band + side, 2 - 2 * turn, turn, whole),
            in_lon_send.at[kind, band],
            in_lon_recv.at[kind, band],
            device(0, 2 * turn - 1),
        )

    def in_lat(kind, col):
        return remote(
            normed,
            (kind, 3 * side, col + turn, both, crossing),
            (kind, 3 - 3 * side, col + turn, both, crossing),
            in_lat_send.at[kind, col],
            in_lat_recv.at[kind, col],
            device(2 * side - 1, 0),
        )

    def in_diag(kind):
        return remote(
            normed,
            (kind, 3 * side, 2 * turn, turn, crossing),
            (kind, 3 - 3 * side, 2 - 2 * turn, turn, crossing),
            in_diag_send.at[kind],
            in_diag_recv.at[kind],
            device(2 * side - 1, 2 * turn - 1),
        )

    def back_lon(kind, band):
        return remote(
            context,
            (kind, band + 1 - side, 2 - 2 * turn, turn, whole),
            (kind, band + 1 - side, 2 * turn, turn, whole),
            back_lon_send.at[kind, band],
            back_lon_recv.at[kind, band],
            device(0, 1 - 2 * turn),
        )

    def back_lat(kind, col):
        return remote(
            context,
            (kind, 3 - 3 * side, col + 1 - turn, both, crossing),
            (kind, 3 * side, col + 1 - turn, both, crossing),
            back_lat_send.at[kind, col],
            back_lat_recv.at[kind, col],
            device(1 - 2 * side, 0),
        )

    def back_diag(kind):
        return remote(
            context,
            (kind, 3 - 3 * side, 2 - 2 * turn, turn, crossing),
            (kind, 3 * side, 2 * turn, turn, crossing),
            back_diag_send.at[kind],
            back_diag_recv.at[kind],
            device(1 - 2 * side, 1 - 2 * turn),
        )

    corner = 1 if side == turn else -1
    neighbours = [(0, 1), (0, -1), (1, 0), (-1, 0), (1, corner), (-1, -corner)]
    barrier = pltpu.get_barrier_semaphore()
    for lat_step, lon_step in neighbours:
        pl.semaphore_signal(
            barrier, inc=1, device_id=device(lat_step, lon_step), device_id_type=MESH
        )

    def prepare(kind, band):
        raws, norms = [], []
        for half in range(2):
            x_copy(kind, half, band).wait()
            raw = x_raw[level_of(kind, half), band].astype(F32)
            raws.append(raw)
            norms.append(norm(raw, ln1_gain[...], ln1_bias[...]))
        parts = []
        for matrix, places in ((split8_ref, range(4)), (split4_ref, range(4, 6))):
            rows = [slice(24 * i, 24 * i + 24) for i in places]
            mixed_rows = [
                jnp.concatenate([level[row] for row in rows for level in levels], axis=0)
                for levels in (raws, norms)
            ]
            parts.append(dot(matrix[...], jnp.concatenate(mixed_rows, axis=1).astype(BF16)))
        for col in range(2):
            halves = []
            for half in range(2):
                place = 2 * col + half
                halves.append(
                    jnp.concatenate(
                        (parts[0][48 * place : 48 * place + 48], parts[1][24 * place : 24 * place + 24]),
                        axis=0,
                    )
                )
                normed[kind, band + side, col + turn, half, :HALF] = halves[half][:, WIDTH:].astype(BF16)
            block = jnp.concatenate([half[:, :WIDTH] for half in halves], axis=0)
            tokens[kind, band, col] = block.astype(BF16)

    def prepare_band(band, carry):
        for kind in range(2):
            prepare(kind, band)

        @pl.when(band == 0)
        def _():
            pl.semaphore_wait(barrier, len(neighbours))

        for kind in range(2):
            in_lon(kind, band).start()
        return carry

    lax.fori_loop(0, 3, prepare_band, 0)
    for kind in range(2):
        in_diag(kind).start()
        in_lat(kind, 0).start()
        in_lat(kind, 1).start()

    def allow(band, carry):
        first = lat * 3 * WIN_LAT + (band - side) * WIN_LAT + lats * 3 * WIN_LAT
        usable = jnp.zeros((UNIT, UNIT), F32)
        for slot in range(WIN_LAT):
            row = first + slot + jnp.where(slot < row_shift, WIN_LAT, 0)
            value = valid_ref[lax.rem(row, lats * 3 * WIN_LAT)].astype(F32)
            usable = jnp.where(pairs_ref[1] == slot, value, usable)
        seam = (lat == 0) & (band == 0) if side else (lat == lats - 1) & (band == 2)
        edge = row_shift.astype(F32)
        query_side = jnp.where(pairs_ref[0] < edge, 1.0, 0.0)
        key_side = jnp.where(pairs_ref[1] < edge, 1.0, 0.0)
        apart = jnp.abs(query_side - key_side) * jnp.where(seam, 1.0, 0.0)
        for kind in range(2):
            serves = (apart < 0.5) & (jnp.maximum(usable, pairs_ref[3]) > 0.5)
            if kind == 1:
                serves = serves & (pairs_ref[2] > 0.5)
            bias[kind, band] = jnp.where(serves, 0.0, -jnp.inf)
        return carry

    lax.fori_loop(0, 3, allow, 0)
    weights[0].wait()

    col_edge = col_shift.astype(F32)

    def pick(ref, kind, band, col, below):
        near, far = (1, 0) if below else (0, 1)
        low_i = lax.broadcasted_iota(jnp.int32, (HALF, WIDTH), 0) < WIN_LON * row_shift
        halves = []
        for half in range(2):

            def across(row):
                low, high = (
                    ref[kind, band + row, col + step, half, :HALF].astype(F32) for step in (near, far)
                )
                if half != turn:
                    return low if turn else high
                return jnp.where(slot_j_ref[...] + 6 * half < col_edge, low, high)

            halves.append(jnp.where(low_i, across(near), across(far)))
        return jnp.concatenate(halves, axis=0).astype(BF16)

    lane = lax.broadcasted_iota(jnp.int32, (UNIT, 128), 1)

    def places_of(rows, cols):
        return [
            (kind, 2 - row if side else row, 1 - col if turn else col)
            for kind in range(2)
            for row, col in zip(rows, cols)
        ]

    def attend_pair(place, item, pair):
        kind, band, col = place
        rows = pl.ds(item * UNIT, UNIT)
        columns = slice(pair * 128, (pair + 1) * 128)
        query = qkv[rows, columns].astype(F32)
        query = jnp.concatenate(
            (jnp.where(lane < 64, query, 0.0), jnp.where(lane < 64, 0.0, query)), axis=0
        ).astype(BF16)
        key = qkv[rows, WIDTH + pair * 128 : WIDTH + (pair + 1) * 128]
        value = qkv[rows, 2 * WIDTH + pair * 128 : 2 * WIDTH + (pair + 1) * 128]
        scores = lax.dot_general(query, key, (((1,), (1,)), ((), ())), preferred_element_type=F32)
        mask = bias[kind, band]
        scores = scores + jnp.concatenate((mask, mask), axis=0)
        top = jnp.max(scores, axis=-1, keepdims=True)
        share = jnp.exp(scores - top).astype(BF16)
        value = jnp.concatenate((value, jnp.ones((UNIT, 128), BF16)), axis=1)
        total = dot(share, value)
        total = total[:, :128] / total[:, 128:]
        total = jnp.where(lane < 64, total[:UNIT], total[UNIT:])
        for half in range(2):
            context[kind, band + 1 - side, col + 1 - turn, half, :HALF, columns] = total[
                half * HALF : (half + 1) * HALF
            ].astype(BF16)

    def attend(stage, carry):
        last = stage // 2

        @pl.when(stage == 1)
        def _():
            for kind in range(2):
                for band in range(3):
                    in_lon(kind, band).wait_recv()

        @pl.when(stage == 2)
        def _():
            for kind in range(2):
                in_lat(kind, 0).wait_recv()
                in_lat(kind, 1).wait_recv()
                in_diag(kind).wait_recv()

        places = places_of(
            [item + last * (2 - item) for item in range(2)],
            [stage * (1 - last) + last * item for item in range(2)],
        )
        window = jnp.concatenate([pick(normed, *place, True) for place in places], axis=0)
        for part in range(3):
            columns = slice(part * WIDTH, (part + 1) * WIDTH)
            value = dot(window, w_qkv[:, columns])
            qkv[:, columns] = (value * 0.125 if part == 0 else value).astype(BF16)
        for item, place in enumerate(places):
            for pair in range(4):
                attend_pair(place, item, pair)

        @pl.when(stage == 1)
        def _():
            for kind, band, _ in places:
                back_lon(kind, band).start()

        @pl.when(stage == 2)
        def _():
            for kind in range(2):
                back_lon(kind, 2 - 2 * side).start()
                back_diag(kind).start()
                back_lat(kind, 0).start()
                back_lat(kind, 1).start()

        return carry

    lax.fori_loop(0, 3, attend, 0)
    for copy in weights[1:4]:
        copy.wait()

    def finish(stage, carry):
        last = stage // 2

        @pl.when(stage == 1)
        def _():
            for kind in range(2):
                for band in range(3):
                    back_lon(kind, band).wait_recv()

        @pl.when(stage == 2)
        def _():
            for kind in range(2):
                back_lat(kind, 0).wait_recv()
                back_lat(kind, 1).wait_recv()
                back_diag(kind).wait_recv()

        places = places_of(
            [(1 + item) * (1 - last) for item in range(2)],
            [(1 - stage) * (1 - last) + last * item for item in range(2)],
        )
        attended = jnp.concatenate([pick(context, *place, False) for place in places], axis=0)
        base = jnp.concatenate([tokens[place] for place in places], axis=0)
        residual = base.astype(F32) + dot(attended, w_proj[...]) + b_proj[...]
        residual = residual.astype(BF16).astype(F32)
        scaled = norm(residual, ln2_gain[...], ln2_bias[...]).astype(BF16)
        for part in range(4):
            columns = slice(part * WIDTH, (part + 1) * WIDTH)
            inner = dot(scaled, w_fc1[:, columns]) + b_fc1[:, columns]
            gelu = 0.5 * inner * (1.0 + lax.erf(inner * np.float32(0.5**0.5)))
            hidden[:, columns] = gelu.astype(BF16)
        total = residual + b_fc2[...] + dot(hidden[...], w_fc2[...])
        total = total.astype(BF16).astype(F32)
        for item, place in enumerate(places):
            mixed[place] = total[item * UNIT : (item + 1) * UNIT]
        return carry

    lax.fori_loop(0, 3, finish, 0)

    def group(band, carry):
        for row in range(3):
            rows = [slice(half * HALF + row * 24, half * HALF + row * 24 + 24) for half in range(2)]
            level = [
                mixed[kind, band, col, part] for kind in range(2) for col in range(2) for part in rows
            ]
            parts = dot(gather_ref[...], jnp.concatenate(level, axis=0).astype(BF16))
            parts = jnp.concatenate([parts[48 * part : 48 * part + 48] for part in range(4)], axis=1)
            grouped[3 * band + row] = norm(parts, merge_gain[...], merge_bias[...]).astype(BF16)
        return carry

    lax.fori_loop(0, 3, group, 0)
    weights[4].wait()

    def merge(part, carry):
        columns = pl.ds(pl.multiple_of(part * 256, 256), 256)
        merged = dot(grouped[...].reshape(432, FF), w_merge[:, columns])
        out_ref[:, columns] = merged.astype(BF16)
        return carry

    lax.fori_loop(0, 4, merge, 0)

    for kind in range(2):
        for band in range(3):
            in_lon(kind, band).wait_send()
            back_lon(kind, band).wait_send()
        for col in range(2):
            in_lat(kind, col).wait_send()
            back_lat(kind, col).wait_send()
        in_diag(kind).wait_send()
        back_diag(kind).wait_send()


def solution(mesh):
    lats, lons = mesh.shape["lat"], mesh.shape["lon"]

    def on_device(
        tokens,
        lat_shift,
        lon_shift,
        lat_valid,
        ln1_gain,
        ln1_bias,
        w_qkv,
        w_proj,
        b_proj,
        ln2_gain,
        ln2_bias,
        w_fc1,
        b_fc1,
        w_fc2,
        b_fc2,
        merge_gain,
        merge_bias,
        w_merge,
    ):
        smem = pl.BlockSpec(memory_space=pltpu.SMEM)
        vmem = pl.BlockSpec(memory_space=pltpu.VMEM)
        hbm = pl.BlockSpec(memory_space=pl.ANY)
        dma = pltpu.SemaphoreType.DMA
        vectors = (
            ln1_gain,
            ln1_bias,
            b_proj,
            ln2_gain,
            ln2_bias,
            b_fc1,
            b_fc2,
            merge_gain,
            merge_bias,
        )
        def variant(side, turn, *operands):
            return pl.pallas_call(
                functools.partial(block_kernel, lats, lons, side, turn),
                out_shape=jax.ShapeDtypeStruct((432, 1024), BF16),
                in_specs=[smem] * 3 + [vmem] * 14 + [hbm] * 6,
                out_specs=vmem,
                scratch_shapes=[
                    pltpu.VMEM((4, 3, UNIT, WIDTH), BF16),
                    pltpu.VMEM((WIDTH, 3 * WIDTH), BF16),
                    pltpu.VMEM((WIDTH, WIDTH), BF16),
                    pltpu.VMEM((WIDTH, FF), BF16),
                    pltpu.VMEM((FF, WIDTH), BF16),
                    pltpu.VMEM((FF, 1024), BF16),
                    pltpu.VMEM((2, 3, 2, UNIT, WIDTH), BF16),
                    pltpu.VMEM((2, 4, 3, 2, ROOM, WIDTH), BF16),
                    pltpu.VMEM((2, 4, 3, 2, ROOM, WIDTH), BF16),
                    pltpu.VMEM((2, 3, 2, UNIT, WIDTH), F32),
                    pltpu.VMEM((2, 3, UNIT, UNIT), F32),
                    pltpu.VMEM((4 * UNIT, 3 * WIDTH), BF16),
                    pltpu.VMEM((4 * UNIT, FF), BF16),
                    pltpu.VMEM((9, 48, FF), BF16),
                    dma((4, 3)),
                    dma((5,)),
                ]
                + [dma((2, 3))] * 2
                + [dma((2, 2))] * 2
                + [dma((2,))] * 2
                + [dma((2, 3))] * 2
                + [dma((2, 2))] * 2
                + [dma((2,))] * 2,
                compiler_params=pltpu.CompilerParams(
                    collective_id=side + 2 * turn, has_side_effects=True, vmem_limit_bytes=58 * 1024 * 1024
                ),
            )(*operands)

        merged = lax.switch(
            jnp.where(lat_shift[0] > 3, 1, 0) + jnp.where(lon_shift[0] > 6, 2, 0),
            [functools.partial(variant, side, turn) for turn in range(2) for side in range(2)],
            lat_shift,
            lon_shift,
            lat_valid,
            *constants(),
            *(vector.reshape(1, -1) for vector in vectors),
            tokens.reshape(4, 3, UNIT, WIDTH),
            w_qkv,
            w_proj,
            w_fc1,
            w_fc2,
            w_merge,
        )
        return merged.reshape(9, 12, 4, 1024).transpose(2, 0, 1, 3)

    return jax.shard_map(
        on_device,
        mesh=mesh,
        in_specs=(P(None, "lat", "lon", None),) + (P(),) * 17,
        out_specs=P(None, "lat", "lon", None),
        check_vma=False,
    )
```
